1024 devices in a mesh: row: 16 (over y, x), col: 64 (over z, core).
Axes of the slice: x: 4, y: 4, z: 32, core: 2. Of those that a mesh axis runs over, the one named last changes fastest.
Arguments:
- features: float32 [131072, 256], P(('col', 'row')), may hold values from -6 to 6
- weight: float32 [256, 128], replicated, may hold values from -0.375 to 0.375
- bias: float32 [128], replicated, may hold values from -3 to 3
- adjacency_tiles: bfloat16 [16, 64, 16, 128, 128], P('row', 'col'), may hold values from -0.046875 to 0.046875
- tile_index: int32 [16, 64, 16], P('row', 'col'), may hold values from 0 to 1023, as said below
- tile_count: int32 [16, 64], P('row', 'col'), may hold values from 1 to 16, as said below
- cotangent: float32 [131072, 128], P(('row', 'col')), may hold values from -6 to 6
Outputs:
- hidden: float32 [131072, 128], P(('row', 'col'))
- grad_features: float32 [131072, 256], P(('col', 'row'))
- grad_weight: float32 [256, 128], replicated
- grad_bias: float32 [128], replicated
The draws below stay inside these ranges and needn't reach their ends.
Inputs may be any that keep to these rules, and one draw needn't show every extreme that they name: `tile_index`: the slots of one block name distinct positions. `tile_count`: some block holds 16 live tiles.
All inputs are finite; a program needn't handle non-finite values.
Results may differ from the reference program's by a relative error of at most 0.013.
Values may be sent and summed in bfloat16 or wider, within the bound.
A program may use at most 64 MiB of HBM per device.

```python
import jax
import jax.numpy as jnp
from jax import lax

F_IN = 256
F = 128
TILE = 128
TROWS = 64
TCOLS = 16
TCAP = 16
NODES = 131072
N_ROW = 16
N_COL = 64


def draw_tile_index(key, part):
    key = jax.random.fold_in(key, 11)
    device_keys = jax.random.split(key, N_ROW * N_COL)
    orders = jax.vmap(lambda single: jax.random.permutation(single, TROWS * TCOLS))(device_keys)
    return orders[:, :TCAP].reshape(N_ROW, N_COL, TCAP).astype(jnp.int32)


def draw_tile_count(key, part):
    key = jax.random.fold_in(key, 23)
    light_key, heavy_key, pick_key, spot_key = jax.random.split(key, 4)
    light = jax.random.randint(light_key, (N_ROW * N_COL,), 1, max(TCAP // 3, 1) + 1)
    heavy = jax.random.randint(heavy_key, (N_ROW * N_COL,), TCAP // 2, TCAP + 1)
    picked = jax.random.randint(pick_key, (N_ROW * N_COL,), 0, 8) == 0
    counts = jnp.where(picked, heavy, light)
    spot = jax.random.randint(spot_key, (), 0, N_ROW * N_COL)
    counts = counts.at[spot].set(TCAP)
    return counts.reshape(N_ROW, N_COL).astype(jnp.int32)


def shard_levels(own_key, shape, shards, least, largest):
    gain, own = 1.0, jax.random.fold_in(own_key, 6)
    for axis_at, blocks in shards:
        heights = jnp.exp(jax.random.uniform(jax.random.fold_in(own, axis_at), (blocks,), jnp.float32, least / len(shards), largest / len(shards)))
        gain = gain * jnp.repeat(heights, shape[axis_at] // blocks).reshape([-1 if axis == axis_at else 1 for axis in range(len(shape))])
    return gain


def gaussian(rng, extent, spread, reach, cuts=(), held_as=jnp.bfloat16):
    drawn = jax.random.normal(rng, extent, jnp.float32) * spread
    if len(cuts) > 0:
        drawn = shard_levels(rng, extent, cuts, -0.22, 0.18) * drawn
    return jnp.clip(drawn, min=-reach, max=reach).astype(held_as)


def setup_inputs(seed: int = 0) -> dict:
    keys = jax.random.split(jax.random.key(seed), 8)
    return {
        "features": gaussian(keys[0], (NODES, F_IN), 1.0, 6.0, ((0, 1024),), jnp.float32),
        "weight": gaussian(keys[1], (F_IN, F), F_IN ** -0.5, 0.375, (), jnp.float32),
        "bias": gaussian(keys[2], (F,), 0.5, 3.0, (), jnp.float32),
        "adjacency_tiles": gaussian(keys[3], (N_ROW, N_COL, TCAP, TILE, TILE), (TILE * N_COL * 2) ** -0.5, 0.046875, ((0, 16), (1, 64))),
        "tile_index": draw_tile_index(jax.random.fold_in(keys[7], 71), 0),
        "tile_count": draw_tile_count(jax.random.fold_in(keys[7], 71), 0),
        "cotangent": gaussian(keys[6], (NODES, F), 1.0, 6.0, ((0, 1024),), jnp.float32),
    }


def gelu_parts(values):
    normal_cdf = 0.5 * (1.0 + jax.scipy.special.erf(values * 0.7071067811865476))
    density = jnp.exp(-0.5 * values * values) * 0.3989422804014327
    return (values * normal_cdf, normal_cdf + values * density)

def reference(features, weight, bias, adjacency_tiles, tile_index, tile_count, cotangent):
    highest = lax.Precision.HIGHEST
    product = jnp.dot(features, weight, precision=highest, preferred_element_type=jnp.float32)
    rounded = lax.optimization_barrier(product.astype(jnp.bfloat16)).astype(jnp.float32)
    panels = rounded.reshape(N_COL, TCOLS, TILE, F)
    slot_ids = jnp.arange(TCAP, dtype=jnp.int32)
    tile_row_ids = jnp.arange(TROWS, dtype=jnp.int32)
    tile_col_ids = jnp.arange(TCOLS, dtype=jnp.int32)

    def forward_block(row_block):

        def over_columns(totals, col_block):
            pieces = adjacency_tiles[row_block, col_block].astype(jnp.float32)
            where = tile_index[row_block, col_block]
            living = (slot_ids < tile_count[row_block, col_block]).astype(jnp.float32)
            gathered = panels[col_block][where % TCOLS]
            products = jnp.einsum('kij,kjf->kif', pieces, gathered, precision=highest) * living[:, None, None]
            onehot = ((where // TCOLS)[:, None] == tile_row_ids[None, :]).astype(jnp.float32)
            return (totals + jnp.einsum('kr,kif->rif', onehot, products, precision=highest), None)
        totals, _ = lax.scan(over_columns, jnp.zeros((TROWS, TILE, F), jnp.float32), jnp.arange(N_COL, dtype=jnp.int32))
        return totals
    aggregated = lax.map(forward_block, jnp.arange(N_ROW, dtype=jnp.int32)).reshape(NODES, F)
    preact = aggregated + bias
    hidden, slopes = gelu_parts(preact)
    grad_preact = cotangent * slopes
    grad_sent = lax.optimization_barrier(grad_preact.astype(jnp.bfloat16)).astype(jnp.float32)
    grad_blocks = grad_sent.reshape(N_ROW, TROWS, TILE, F)

    def backward_block(col_block):

        def over_rows(totals, row_block):
            pieces = adjacency_tiles[row_block, col_block].astype(jnp.float32)
            where = tile_index[row_block, col_block]
            living = (slot_ids < tile_count[row_block, col_block]).astype(jnp.float32)
            gathered = grad_blocks[row_block][where // TCOLS]
            products = jnp.einsum('kji,kjf->kif', pieces, gathered, precision=highest) * living[:, None, None]
            onehot = ((where % TCOLS)[:, None] == tile_col_ids[None, :]).astype(jnp.float32)
            term = jnp.einsum('kc,kif->cif', onehot, products, precision=highest)
            term = lax.optimization_barrier(term.astype(jnp.bfloat16)).astype(jnp.float32)
            return (totals + term, None)
        totals, _ = lax.scan(over_rows, jnp.zeros((TCOLS, TILE, F), jnp.float32), jnp.arange(N_ROW, dtype=jnp.int32))
        return totals
    grad_product = lax.map(backward_block, jnp.arange(N_COL, dtype=jnp.int32)).reshape(NODES, F)
    grad_features = jnp.dot(grad_product, weight.T, precision=highest, preferred_element_type=jnp.float32)
    scaling = 1.0 / jnp.sqrt(jnp.float32(NODES))
    grad_weight = jnp.dot(features.T, grad_product, precision=highest, preferred_element_type=jnp.float32) * scaling
    grad_bias = lax.optimization_barrier(jnp.sum(grad_preact, axis=0)) * scaling
    return (hidden, grad_features, grad_weight, grad_bias)
```

```python
import functools
import math

import jax
import jax.numpy as jnp
from jax import lax
from jax.experimental import pallas as pl
from jax.experimental.pallas import tpu as pltpu
from jax.sharding import PartitionSpec as P

F32, BF16 = jnp.float32, jnp.bfloat16
HIGHEST = lax.Precision.HIGHEST


def gelu_parts(values):
    normal_cdf = 0.5 * (1.0 + lax.erf(values * 0.7071067811865476))
    density = jnp.exp(-0.5 * values * values) * 0.3989422804014327
    return (values * normal_cdf, normal_cdf + values * density)


def layer(
    n_row,
    nz,
    scaling,
    where,
    live,
    features,
    weight,
    bias,
    cotangent,
    tiles_hbm,
    hidden_out,
    grad_features_out,
    grad_weight_out,
    grad_bias_out,
    tiles,
    tiles_t,
    features_t,
    panel,
    products,
    compact,
    to_sib,
    from_sib,
    up,
    down,
    grads,
    back,
    back_in,
    terms,
    terms_in,
    near,
    far,
    total,
    prev_row,
    prev_col,
    last_row,
    last_col,
    tile_sem,
    panel_send,
    panel_recv,
    sib_send,
    sib_recv,
    up_send,
    up_recv,
    down_send,
    down_recv,
    right_send,
    right_recv,
    left_send,
    left_recv,
    pass_send,
    pass_recv,
    back_send,
    back_recv,
    terms_send,
    terms_recv,
    near_send,
    near_recv,
    far_send,
    far_recv,
    total_send,
    total_recv,
):
    slots = tiles.shape[0]
    row, col = lax.axis_index("row"), lax.axis_index("col")
    z, core = col // 2, col % 2
    half = nz // 2
    near_n = math.gcd(8, nz) if nz >= 16 else 2
    far_n = nz // near_n
    n_plane = 2 * n_row
    place = 2 * row + core
    group, spot = z // near_n, z % near_n

    def device(at_row, at_z, at_core):
        return (at_row, 2 * at_z + at_core)

    def remote(src, dst, send, recv, to):
        return pltpu.make_async_remote_copy(
            src_ref=src,
            dst_ref=dst,
            send_sem=send,
            recv_sem=recv,
            device_id=to,
            device_id_type=pl.DeviceIdType.MESH,
        )

    def settle(ref, sem):
        pltpu.make_async_copy(ref, ref, sem).wait()

    right = device(row, (z + 1) % nz, core)
    left = device(row, (z + nz - 1) % nz, core)
    sibling = device(row, z, 1 - core)

    def plane(step):
        other = (place + step) % n_plane
        return device(other // 2, z, other % 2), other

    def near_peer(step):
        return device(row, group * near_n + (spot + step) % near_n, core)

    def far_peer(step):
        return device(row, (z + near_n * step) % nz, core)

    barrier = pltpu.get_barrier_semaphore()

    def greet(to):
        pl.semaphore_signal(
            barrier, inc=1, device_id=to, device_id_type=pl.DeviceIdType.MESH
        )

    @pl.loop(1, n_plane)
    def _(step):
        greet(plane(step)[0])

    @pl.loop(1, near_n)
    def _(step):
        greet(near_peer(step))

    @pl.loop(1, far_n)
    def _(step):
        greet(far_peer(step))

    greet(right)
    greet(left)

    tile_copy = pltpu.make_async_copy(tiles_hbm, tiles, tile_sem)
    tile_copy.start()
    panel[row] = jnp.dot(
        features[...], weight[...], precision=HIGHEST, preferred_element_type=F32
    ).astype(BF16)
    pl.semaphore_wait(barrier, n_plane - 1 + near_n - 1 + far_n - 1 + 2)

    def panel_copy(step):
        return remote(
            panel.at[row],
            panel.at[row],
            panel_send.at[step],
            panel_recv.at[step],
            device((row + step) % n_row, z, core),
        )

    @pl.loop(1, n_row)
    def _(step):
        panel_copy(step).start()

    count = live[0]
    n_cols = n_row

    @pl.loop(0, slots)
    def _(slot):
        mine = where[slot]
        by_row, by_col = jnp.int32(slots), jnp.int32(slots)
        for other in range(slots):
            theirs = where[other]
            before = other < slot
            by_row = jnp.where(
                before & (theirs // n_cols == mine // n_cols), other, by_row
            )
            by_col = jnp.where(
                before & (theirs % n_cols == mine % n_cols), other, by_col
            )
        prev_row[slot] = by_row
        prev_col[slot] = by_col

    @pl.loop(0, 2 * nz)
    def _(tile_row):
        last = jnp.int32(slots)
        for other in range(slots):
            last = jnp.where(
                (other < count) & (where[other] // n_cols == tile_row), other, last
            )
        last_row[tile_row] = last

    @pl.loop(0, n_cols)
    def _(tile_col):
        last = jnp.int32(slots)
        for other in range(slots):
            last = jnp.where(
                (other < count) & (where[other] % n_cols == tile_col), other, last
            )
        last_col[tile_col] = last

    products[slots] = jnp.zeros_like(products[slots])
    compact[slots] = jnp.zeros_like(compact[slots])
    tile_copy.wait()

    @pl.loop(1, n_row)
    def _(step):
        panel_copy(step).wait_recv()

    for slot in range(slots):
        products[slot] = jnp.dot(
            tiles[slot], panel[where[slot] % n_cols], preferred_element_type=F32
        )

    @pl.loop(0, slots)
    def _(slot):
        added = products[slot] + products[prev_row[slot]]
        products[slot] = added
        compact[slot] = added.astype(BF16)

    parts = sib_send.shape[0] // 2
    width = half // parts

    def sib_copies(part):
        for end, first in enumerate((part * width, nz - width - part * width)):
            yield remote(
                to_sib.at[pl.ds(first, width)],
                from_sib.at[pl.ds(first, width)],
                sib_send.at[2 * part + end],
                sib_recv.at[2 * part + end],
                sibling,
            )

    def slot_of(at, whose):
        return last_row[2 * ((z + at + nz - (half - 1)) % nz) + whose]

    for part in range(parts):

        @pl.loop(part * width, (part + 1) * width)
        def _(at):
            to_sib[at] = compact[slot_of(at, 1 - core)]
            to_sib[nz - 1 - at] = compact[slot_of(nz - 1 - at, 1 - core)]

        for copy in sib_copies(part):
            copy.start()

    def up_copy(step):
        return remote(up.at[step], up.at[step + 1], up_send, up_recv.at[step], right)

    def down_copy(step):
        return remote(
            down.at[step], down.at[step + 1], down_send, down_recv.at[step], left
        )

    def chip_part(at):
        return compact[slot_of(at, core)].astype(F32) + from_sib[at].astype(F32)

    for part in range(parts):
        for copy in sib_copies(part):
            copy.wait_recv()
        if part == 0:
            up[0] = chip_part(nz - 1).astype(BF16)
            up_copy(0).start()
            down[0] = chip_part(0).astype(BF16)
            down_copy(0).start()

        @pl.loop(max(1, part * width), (part + 1) * width)
        def _(step):
            mine = chip_part(nz - 1 - step)
            up_copy(step - 1).wait_recv()
            up[step] = (up[step].astype(F32) + mine).astype(BF16)
            up_copy(step).start()

            @pl.when(step < half - 1)
            def _():
                mine = chip_part(step)
                down_copy(step - 1).wait_recv()
                down[step] = (down[step].astype(F32) + mine).astype(BF16)
                down_copy(step).start()

    own = products[slot_of(half - 1, core)] + from_sib[half - 1].astype(F32)
    own = own + bias[...]
    down_copy(half - 2).wait_recv()
    own = own + down[half - 1].astype(F32)
    up_copy(half - 1).wait_recv()
    preact = own + up[half].astype(F32)
    hidden, slopes = gelu_parts(preact)
    grad_preact = cotangent[...] * slopes
    grads[core, z] = grad_preact.astype(BF16)

    def right_copy(step):
        at = grads.at[core, (z + nz - step) % nz]
        return remote(at, at, right_send, right_recv.at[step], right)

    def left_copy(step):
        at = grads.at[core, (z + step) % nz]
        return remote(at, at, left_send, left_recv.at[step], left)

    def pass_copy(at_z):
        at = grads.at[core, at_z]
        return remote(at, at, pass_send, pass_recv, sibling)

    right_copy(0).start()
    left_copy(0).start()
    pass_copy(z).start()
    hidden_out[...] = hidden
    rows_dev, width_out = grad_preact.shape
    bias_term = jnp.sum(grad_preact.reshape(rows_dev // 8, 8, width_out), axis=0)

    @pl.loop(0, n_plane)
    def _(at):
        terms[at, 8:16] = bias_term

    @pl.loop(0, slots)
    def _(slot):
        tiles_t[slot] = tiles[slot].T

    features_t[...] = features[...].T


    @pl.loop(0, half)
    def _(step):
        from_left = (z + nz - 1 - step) % nz
        right_copy(step).wait_recv()

        @pl.when(step < half - 1)
        def _():
            right_copy(step + 1).start()

        pass_copy(from_left).start()

        @pl.when(step < half - 1)
        def _():
            from_right = (z + 1 + step) % nz
            left_copy(step).wait_recv()

            @pl.when(step < half - 2)
            def _():
                left_copy(step + 1).start()

            pass_copy(from_right).start()

    settle(grads.at[1 - core], pass_recv)

    for slot in range(slots):
        tile_row = where[slot] // n_cols
        products[slot] = jnp.dot(
            tiles_t[slot],
            grads[tile_row % 2, tile_row // 2],
            preferred_element_type=F32,
        )

    @pl.loop(0, slots)
    def _(slot):
        products[slot] = products[slot] + products[prev_col[slot]]

    def back_copy(step):
        to = (row + step) % n_row
        return remote(
            back.at[step],
            back_in.at[step],
            back_send.at[step],
            back_recv.at[step],
            device(to, z, core),
        )

    @pl.loop(1, n_row)
    def _(step):
        back[step] = products[last_col[(row + step) % n_row]].astype(BF16)
        back_copy(step).start()

    products[slots] = products[last_col[row]].astype(BF16).astype(F32)

    @pl.loop(1, n_row)
    def _(step):
        back_copy(step).wait_recv()
        products[slots] = products[slots] + back_in[step].astype(F32)

    grad_product = products[slots]

    weight_term = jnp.dot(
        features_t[...], grad_product, precision=HIGHEST, preferred_element_type=F32
    )
    for at in range(n_plane):
        terms[at, 0:8] = weight_term[8 * at : 8 * at + 8]

    def terms_copy(step):
        to, other = plane(step)
        return remote(
            terms.at[other],
            terms_in.at[place],
            terms_send.at[step],
            terms_recv.at[step],
            to,
        )

    @pl.loop(1, n_plane)
    def _(step):
        terms_copy(step).start()

    grad_features_out[...] = lax.dot_general(
        grad_product,
        weight[...],
        (((1,), (1,)), ((), ())),
        precision=HIGHEST,
        preferred_element_type=F32,
    )
    terms_in[place] = terms[place]

    @pl.loop(1, n_plane)
    def _(step):
        terms_copy(step).wait_recv()

    near[spot] = lax.fori_loop(
        1, n_plane, lambda at, so_far: so_far + terms_in[at], terms_in[0]
    )

    def near_copy(step):
        return remote(
            near.at[spot],
            near.at[spot],
            near_send.at[step],
            near_recv.at[step],
            near_peer(step),
        )

    def far_copy(step):
        return remote(
            far.at[group],
            far.at[group],
            far_send.at[step],
            far_recv.at[step],
            far_peer(step),
        )

    for step in range(1, near_n):
        near_copy(step).start()
    for step in range(1, near_n):
        near_copy(step).wait_recv()
    far[group] = sum((near[at] for at in range(1, near_n)), near[0])
    for step in range(1, far_n):
        far_copy(step).start()
    for step in range(1, far_n):
        far_copy(step).wait_recv()
    summed = sum((far[at] for at in range(1, far_n)), far[0]) * scaling
    total[place] = summed[0:8]

    def total_copy(step):
        return remote(
            total.at[place],
            total.at[place],
            total_send.at[step],
            total_recv.at[step],
            plane(step)[0],
        )

    @pl.loop(1, n_plane)
    def _(step):
        total_copy(step).start()

    grad_bias_out[...] = jnp.sum(summed[8:16], axis=0, keepdims=True)

    @pl.loop(1, n_row)
    def _(step):
        panel_copy(step).wait_send()
        back_copy(step).wait_send()

    for part in range(parts):
        for copy in sib_copies(part):
            copy.wait_send()
    settle(up.at[pl.ds(0, half)], up_send)
    settle(down.at[pl.ds(0, half - 1)], down_send)
    settle(grads.at[0, pl.ds(0, half)], right_send)
    settle(grads.at[0, pl.ds(0, half - 1)], left_send)
    settle(grads.at[0], pass_send)

    @pl.loop(1, n_plane)
    def _(step):
        terms_copy(step).wait_send()

    for step in range(1, near_n):
        near_copy(step).wait_send()
    for step in range(1, far_n):
        far_copy(step).wait_send()

    @pl.loop(1, n_plane)
    def _(step):
        total_copy(step).wait_recv()

    grad_weight_out[...] = total[...]

    @pl.loop(1, n_plane)
    def _(step):
        total_copy(step).wait_send()


def local(n_row, n_col, features, weight, bias, tiles, where, live, cotangent):
    slots, tile = tiles.shape[2], tiles.shape[3]
    rows_dev, f_in = features.shape
    f_out = weight.shape[1]
    nz = n_col // 2
    half = nz // 2
    near_n = math.gcd(8, nz) if nz >= 16 else 2
    far_n = nz // near_n
    n_plane = 2 * n_row
    parts = min(4, half)
    nodes = rows_dev * n_row * n_col
    chunk = f_in // n_plane
    assert chunk == 8 and rows_dev == tile
    dma = pltpu.SemaphoreType.DMA
    vmem = pl.BlockSpec(memory_space=pltpu.VMEM)
    smem = pl.BlockSpec(memory_space=pltpu.SMEM)
    hidden, grad_features, grad_weight, grad_bias = pl.pallas_call(
        functools.partial(layer, n_row, nz, 1.0 / math.sqrt(nodes)),
        out_shape=(
            jax.ShapeDtypeStruct((rows_dev, f_out), F32),
            jax.ShapeDtypeStruct((rows_dev, f_in), F32),
            jax.ShapeDtypeStruct((n_plane, chunk, f_out), F32),
            jax.ShapeDtypeStruct((1, f_out), F32),
        ),
        in_specs=[smem, smem, vmem, vmem, vmem, vmem, pl.BlockSpec(memory_space=pl.ANY)],
        out_specs=(vmem, vmem, vmem, vmem),
        scratch_shapes=[
            pltpu.VMEM((slots, tile, tile), BF16),
            pltpu.VMEM((slots, tile, tile), BF16),
            pltpu.VMEM((f_in, rows_dev), F32),
            pltpu.VMEM((n_row, tile, f_out), BF16),
            pltpu.VMEM((slots + 1, tile, f_out), F32),
            pltpu.VMEM((slots + 1, tile, f_out), BF16),
            pltpu.VMEM((nz, tile, f_out), BF16),
            pltpu.VMEM((nz, tile, f_out), BF16),
            pltpu.VMEM((half + 1, tile, f_out), BF16),
            pltpu.VMEM((half, tile, f_out), BF16),
            pltpu.VMEM((2, nz, tile, f_out), BF16),
            pltpu.VMEM((n_row, tile, f_out), BF16),
            pltpu.VMEM((n_row, tile, f_out), BF16),
            pltpu.VMEM((n_plane, 2 * chunk, f_out), F32),
            pltpu.VMEM((n_plane, 2 * chunk, f_out), F32),
            pltpu.VMEM((near_n, 2 * chunk, f_out), F32),
            pltpu.VMEM((far_n, 2 * chunk, f_out), F32),
            pltpu.VMEM((n_plane, chunk, f_out), F32),
            pltpu.SMEM((slots,), jnp.int32),
            pltpu.SMEM((slots,), jnp.int32),
            pltpu.SMEM((n_col,), jnp.int32),
            pltpu.SMEM((n_row,), jnp.int32),
            dma,
            dma((n_row,)),
            dma((n_row,)),
            dma((2 * parts,)),
            dma((2 * parts,)),
            dma,
            dma((half,)),
            dma,
            dma((half,)),
            dma,
            dma((half,)),
            dma,
            dma((half,)),
            dma,
            dma,
            dma((n_row,)),
            dma((n_row,)),
            dma((n_plane,)),
            dma((n_plane,)),
            dma((near_n,)),
            dma((near_n,)),
            dma((far_n,)),
            dma((far_n,)),
            dma((n_plane,)),
            dma((n_plane,)),
        ],
        compiler_params=pltpu.CompilerParams(
            collective_id=0, has_side_effects=True, vmem_limit_bytes=48 * 1024 * 1024
        ),
    )(
        where.reshape(slots),
        live.reshape(1),
        features,
        weight,
        bias.reshape(1, f_out),
        cotangent,
        tiles.reshape(slots, tile, tile),
    )
    return (
        hidden,
        grad_features,
        grad_weight.reshape(f_in, f_out),
        grad_bias.reshape(f_out),
    )


def solution(mesh):
    placed = (
        P(("col", "row"), None),
        P(),
        P(),
        P("row", "col", None, None, None),
        P("row", "col", None),
        P("row", "col"),
        P(("row", "col"), None),
    )
    return jax.shard_map(
        functools.partial(local, mesh.shape["row"], mesh.shape["col"]),
        mesh=mesh,
        in_specs=placed,
        out_specs=(P(("row", "col"), None), P(("col", "row"), None), P(), P()),
        check_vma=False,
    )
```

```python
import functools
import math

import jax
import jax.numpy as jnp
from jax import lax
from jax.experimental import pallas as pl
from jax.experimental.pallas import tpu as pltpu
from jax.sharding import PartitionSpec as P

F32, BF16 = jnp.float32, jnp.bfloat16
HIGHEST = lax.Precision.HIGHEST


def plan(nz):
    half = nz // 2
    stride = 4 if half % 4 == 0 and half > 4 else 2
    near_n = 8 if nz % 8 == 0 and nz > 8 else 2
    return half, stride, half // stride, near_n, nz // near_n


def gelu_parts(values):
    normal_cdf = 0.5 * (1.0 + lax.erf(values * 0.7071067811865476))
    density = jnp.exp(-0.5 * values * values) * 0.3989422804014327
    return (values * normal_cdf, normal_cdf + values * density)


def layer(
    n_row,
    nz,
    scaling,
    where,
    live,
    features_hbm,
    weight_hbm,
    bias_hbm,
    cotangent_hbm,
    tiles_hbm,
    hidden_out,
    grad_features_out,
    grad_weight_out,
    grad_bias_out,
    features,
    weight,
    bias,
    cotangent,
    tiles,
    tiles_t,
    features_t,
    panel,
    products,
    compact,
    to_sib,
    from_sib,
    up,
    down,
    up_in,
    down_in,
    grads,
    back,
    back_in,
    terms,
    terms_in,
    near,
    far,
    total,
    prev_row,
    prev_col,
    last_row,
    last_col,
    load_sem,
    panel_send,
    panel_recv,
    sib_send,
    sib_recv,
    up_send,
    up_recv,
    down_send,
    down_recv,
    right_send,
    right_recv,
    left_send,
    left_recv,
    pass_send,
    pass_recv,
    back_send,
    back_recv,
    terms_send,
    terms_recv,
    near_send,
    near_recv,
    far_send,
    far_recv,
    total_send,
    total_recv,
):
    slots = tiles.shape[0]
    row, col = lax.axis_index("row"), lax.axis_index("col")
    z, core = col // 2, col % 2
    half, stride, levels, near_n, far_n = plan(nz)
    n_plane = 2 * n_row
    place = 2 * row + core
    group, spot = z // near_n, z % near_n

    def device(at_row, at_z, at_core):
        return (at_row, 2 * at_z + at_core)

    def remote(src, dst, send, recv, to):
        return pltpu.make_async_remote_copy(
            src_ref=src,
            dst_ref=dst,
            send_sem=send,
            recv_sem=recv,
            device_id=to,
            device_id_type=pl.DeviceIdType.MESH,
        )

    def settle(ref, sem):
        pltpu.make_async_copy(ref, ref, sem).wait()

    def above(hop):
        return device(row, (z + hop) % nz, core)

    def below(hop):
        return device(row, (z + nz - hop) % nz, core)

    sibling = device(row, z, 1 - core)

    def plane(step):
        other = (place + step) % n_plane
        return device(other // 2, z, other % 2), other

    def near_peer(step):
        return device(row, group * near_n + (spot + step) % near_n, core)

    def far_peer(step):
        return device(row, (z + near_n * step) % nz, core)

    barrier = pltpu.get_barrier_semaphore()

    def greet(to):
        pl.semaphore_signal(
            barrier, inc=1, device_id=to, device_id_type=pl.DeviceIdType.MESH
        )

    for hop in range(1, stride + 1):
        greet(above(hop))
        greet(below(hop))

    @pl.loop(1, n_plane)
    def _(step):
        greet(plane(step)[0])

    loads = [
        pltpu.make_async_copy(src, dst, load_sem.at[at])
        for at, (src, dst) in enumerate(
            (
                (features_hbm, features),
                (weight_hbm, weight),
                (tiles_hbm, tiles),
                (bias_hbm, bias),
                (cotangent_hbm, cotangent),
            )
        )
    ]
    for load in loads:
        load.start()
    loads[0].wait()
    loads[1].wait()
    panel[row] = jnp.dot(
        features[...], weight[...], precision=HIGHEST, preferred_element_type=F32
    ).astype(BF16)
    pl.semaphore_wait(barrier, n_plane - 1 + 2 * stride)

    def panel_copy(step):
        return remote(
            panel.at[row],
            panel.at[row],
            panel_send.at[step],
            panel_recv.at[step],
            device((row + step) % n_row, z, core),
        )

    @pl.loop(1, n_row)
    def _(step):
        panel_copy(step).start()

    count = live[0]
    n_cols = n_row

    @pl.loop(0, slots)
    def _(slot):
        mine = where[slot]
        by_row, by_col = jnp.int32(slots), jnp.int32(slots)
        for other in range(slots):
            theirs = where[other]
            before = other < slot
            by_row = jnp.where(
                before & (theirs // n_cols == mine // n_cols), other, by_row
            )
            by_col = jnp.where(
                before & (theirs % n_cols == mine % n_cols), other, by_col
            )
        prev_row[slot] = by_row
        prev_col[slot] = by_col

    @pl.loop(0, 2 * nz)
    def _(tile_row):
        last = jnp.int32(slots)
        for other in range(slots):
            last = jnp.where(
                (other < count) & (where[other] // n_cols == tile_row), other, last
            )
        last_row[tile_row] = last

    @pl.loop(0, n_cols)
    def _(tile_col):
        last = jnp.int32(slots)
        for other in range(slots):
            last = jnp.where(
                (other < count) & (where[other] % n_cols == tile_col), other, last
            )
        last_col[tile_col] = last

    products[slots] = jnp.zeros_like(products[slots])
    compact[slots] = jnp.zeros_like(compact[slots])
    for load in loads[2:]:
        load.wait()

    @pl.loop(1, n_row)
    def _(step):
        panel_copy(step).wait_recv()

    for slot in range(slots):
        products[slot] = jnp.dot(
            tiles[slot], panel[where[slot] % n_cols], preferred_element_type=F32
        )

    @pl.loop(0, slots)
    def _(slot):
        added = products[slot] + products[prev_row[slot]]
        products[slot] = added
        compact[slot] = added.astype(BF16)

    parts, width = levels, stride

    def sib_copies(part):
        for end, first in enumerate((part * width, nz - width - part * width)):
            yield remote(
                to_sib.at[pl.ds(first, width)],
                from_sib.at[pl.ds(first, width)],
                sib_send.at[2 * part + end],
                sib_recv.at[2 * part + end],
                sibling,
            )

    def slot_of(at, whose):
        return last_row[2 * ((z + at + nz - (half - 1)) % nz) + whose]

    for part in range(parts):

        @pl.loop(part * width, (part + 1) * width)
        def _(at):
            to_sib[at] = compact[slot_of(at, 1 - core)]
            to_sib[nz - 1 - at] = compact[slot_of(nz - 1 - at, 1 - core)]

        for copy in sib_copies(part):
            copy.start()

    def up_copy(dist):
        to = above(dist % stride or stride)
        return remote(up.at[dist], up_in.at[dist], up_send, up_recv.at[dist], to)

    def down_copy(dist):
        to = below(dist % stride or stride)
        return remote(
            down.at[dist], down_in.at[dist], down_send, down_recv.at[dist], to
        )

    def chip_part(dist):
        at = half - 1 + dist
        return compact[slot_of(at, core)].astype(F32) + from_sib[at].astype(F32)

    def send_up(dist, value):
        up[dist] = value.astype(BF16)
        up_copy(dist).start()

    def send_down(dist, value):
        down[dist] = value.astype(BF16)
        down_copy(dist).start()

    def fill(level):
        for copy in sib_copies(levels - 1 - level):
            copy.wait_recv()
        if level == levels - 1:
            send_up(half, chip_part(half))
        for hop in range(stride - 1, 0, -1):
            dist = level * stride + hop
            send_down(dist, chip_part(-dist))
            send_up(dist, chip_part(dist))

    def gather_up(level, value):
        for dist in range(level * stride + 1, (level + 1) * stride + 1):
            up_copy(dist).wait_recv()
            value = value + up_in[dist].astype(F32)
        return value

    def gather_down(level, value):
        for dist in range(level * stride + 1, min((level + 1) * stride, half - 1) + 1):
            down_copy(dist).wait_recv()
            value = value + down_in[dist].astype(F32)
        return value

    fill(levels - 1)
    for level in range(levels - 1, 0, -1):
        fill(level - 1)
        dist = level * stride
        send_up(dist, gather_up(level, chip_part(dist)))
        send_down(dist, gather_down(level, chip_part(-dist)))

    own = products[slot_of(half - 1, core)] + from_sib[half - 1].astype(F32)
    preact = gather_up(0, gather_down(0, own + bias[...]))
    hidden, slopes = gelu_parts(preact)
    grad_preact = cotangent[...] * slopes
    grads[core, z] = grad_preact.astype(BF16)

    def right_copy(level, hop):
        at = grads.at[core, (z + nz - level * stride) % nz]
        sem = right_recv.at[level * stride + hop]
        return remote(at, at, right_send, sem, above(hop))

    def left_copy(level, hop):
        at = grads.at[core, (z + level * stride) % nz]
        sem = left_recv.at[level * stride + hop]
        return remote(at, at, left_send, sem, below(hop))

    def pass_copy(at_z):
        at = grads.at[core, at_z]
        return remote(at, at, pass_send, pass_recv, sibling)

    def from_left(dist):
        at = (z + nz - dist) % nz
        settle(grads.at[core, at], right_recv.at[dist])
        return at

    def from_right(dist):
        at = (z + dist) % nz
        settle(grads.at[core, at], left_recv.at[dist])
        return at

    right_copy(0, stride).start()
    left_copy(0, stride).start()
    for hop in range(stride - 1, 0, -1):
        right_copy(0, hop).start()
        left_copy(0, hop).start()
    pass_copy(z).start()
    hidden_out[...] = hidden
    rows_dev, width_out = grad_preact.shape
    bias_term = jnp.sum(grad_preact.reshape(rows_dev // 8, 8, width_out), axis=0)

    @pl.loop(0, n_plane)
    def _(at):
        terms[at, 8:16] = bias_term

    @pl.loop(0, slots)
    def _(slot):
        tiles_t[slot] = tiles[slot].T

    features_t[...] = features[...].T


    for level in range(1, levels + 1):
        relayed = [from_left(level * stride)]
        if level < levels:
            right_copy(level, stride).start()
            relayed.append(from_right(level * stride))
            if level < levels - 1:
                left_copy(level, stride).start()
            for hop in range(stride - 1, 0, -1):
                right_copy(level, hop).start()
                left_copy(level, hop).start()
        for at in relayed:
            pass_copy(at).start()
        for hop in range(1, stride):
            dist = (level - 1) * stride + hop
            pass_copy(from_left(dist)).start()
            pass_copy(from_right(dist)).start()

    settle(grads.at[1 - core], pass_recv)

    for slot in range(slots):
        tile_row = where[slot] // n_cols
        products[slot] = jnp.dot(
            tiles_t[slot],
            grads[tile_row % 2, tile_row // 2],
            preferred_element_type=F32,
        )

    @pl.loop(0, slots)
    def _(slot):
        products[slot] = products[slot] + products[prev_col[slot]]

    def back_copy(step):
        to = (row + step) % n_row
        return remote(
            back.at[step],
            back_in.at[step],
            back_send.at[step],
            back_recv.at[step],
            device(to, z, core),
        )

    @pl.loop(1, n_row)
    def _(step):
        back[step] = products[last_col[(row + step) % n_row]].astype(BF16)
        back_copy(step).start()

    products[slots] = products[last_col[row]].astype(BF16).astype(F32)

    @pl.loop(1, n_row)
    def _(step):
        back_copy(step).wait_recv()
        products[slots] = products[slots] + back_in[step].astype(F32)

    grad_product = products[slots]

    weight_term = jnp.dot(
        features_t[...], grad_product, precision=HIGHEST, preferred_element_type=F32
    )
    for at in range(n_plane):
        terms[at, 0:8] = weight_term[8 * at : 8 * at + 8]

    def terms_copy(step):
        to, other = plane(step)
        return remote(
            terms.at[other],
            terms_in.at[place],
            terms_send.at[step],
            terms_recv.at[step],
            to,
        )

    @pl.loop(1, n_plane)
    def _(step):
        terms_copy(step).start()

    grad_features_out[...] = lax.dot_general(
        grad_product,
        weight[...],
        (((1,), (1,)), ((), ())),
        precision=HIGHEST,
        preferred_element_type=F32,
    )
    terms_in[place] = terms[place]

    @pl.loop(1, n_plane)
    def _(step):
        terms_copy(step).wait_recv()

    near[spot] = lax.fori_loop(
        1, n_plane, lambda at, so_far: so_far + terms_in[at], terms_in[0]
    )

    def near_copy(step):
        return remote(
            near.at[spot],
            near.at[spot],
            near_send.at[step],
            near_recv.at[step],
            near_peer(step),
        )

    def far_copy(step):
        return remote(
            far.at[group],
            far.at[group],
            far_send.at[step],
            far_recv.at[step],
            far_peer(step),
        )

    for step in range(1, near_n):
        near_copy(step).start()
    for step in range(1, near_n):
        near_copy(step).wait_recv()
    far[group] = sum((near[at] for at in range(1, near_n)), near[0])
    for step in range(1, far_n):
        far_copy(step).start()
    for step in range(1, far_n):
        far_copy(step).wait_recv()
    summed = sum((far[at] for at in range(1, far_n)), far[0]) * scaling
    total[place] = summed[0:8]

    def total_copy(step):
        return remote(
            total.at[place],
            total.at[place],
            total_send.at[step],
            total_recv.at[step],
            plane(step)[0],
        )

    @pl.loop(1, n_plane)
    def _(step):
        total_copy(step).start()

    grad_bias_out[...] = jnp.sum(summed[8:16], axis=0, keepdims=True)

    @pl.loop(1, n_row)
    def _(step):
        panel_copy(step).wait_send()
        back_copy(step).wait_send()

    for part in range(parts):
        for copy in sib_copies(part):
            copy.wait_send()
    settle(up.at[pl.ds(1, half)], up_send)
    settle(down.at[pl.ds(1, half - 1)], down_send)
    settle(grads.at[0, pl.ds(0, half)], right_send)
    settle(grads.at[0, pl.ds(0, half - 1)], left_send)
    settle(grads.at[0], pass_send)

    @pl.loop(1, n_plane)
    def _(step):
        terms_copy(step).wait_send()

    for step in range(1, near_n):
        near_copy(step).wait_send()
    for step in range(1, far_n):
        far_copy(step).wait_send()

    @pl.loop(1, n_plane)
    def _(step):
        total_copy(step).wait_recv()

    grad_weight_out[...] = total[...]

    @pl.loop(1, n_plane)
    def _(step):
        total_copy(step).wait_send()


def local(n_row, n_col, features, weight, bias, tiles, where, live, cotangent):
    slots, tile = tiles.shape[2], tiles.shape[3]
    rows_dev, f_in = features.shape
    f_out = weight.shape[1]
    nz = n_col // 2
    half, stride, levels, near_n, far_n = plan(nz)
    n_plane = 2 * n_row
    parts = levels
    nodes = rows_dev * n_row * n_col
    chunk = f_in // n_plane
    assert chunk == 8 and rows_dev == tile
    dma = pltpu.SemaphoreType.DMA
    vmem = pl.BlockSpec(memory_space=pltpu.VMEM)
    smem = pl.BlockSpec(memory_space=pltpu.SMEM)
    hidden, grad_features, grad_weight, grad_bias = pl.pallas_call(
        functools.partial(layer, n_row, nz, 1.0 / math.sqrt(nodes)),
        out_shape=(
            jax.ShapeDtypeStruct((rows_dev, f_out), F32),
            jax.ShapeDtypeStruct((rows_dev, f_in), F32),
            jax.ShapeDtypeStruct((n_plane, chunk, f_out), F32),
            jax.ShapeDtypeStruct((1, f_out), F32),
        ),
        in_specs=[smem, smem] + [pl.BlockSpec(memory_space=pl.ANY)] * 5,
        out_specs=(vmem, vmem, vmem, vmem),
        scratch_shapes=[
            pltpu.VMEM(features.shape, F32),
            pltpu.VMEM(weight.shape, F32),
            pltpu.VMEM((1, f_out), F32),
            pltpu.VMEM(cotangent.shape, F32),
            pltpu.VMEM((slots, tile, tile), BF16),
            pltpu.VMEM((slots, tile, tile), BF16),
            pltpu.VMEM((f_in, rows_dev), F32),
            pltpu.VMEM((n_row, tile, f_out), BF16),
            pltpu.VMEM((slots + 1, tile, f_out), F32),
            pltpu.VMEM((slots + 1, tile, f_out), BF16),
            pltpu.VMEM((nz, tile, f_out), BF16),
            pltpu.VMEM((nz, tile, f_out), BF16),
            pltpu.VMEM((half + 1, tile, f_out), BF16),
            pltpu.VMEM((half + 1, tile, f_out), BF16),
            pltpu.VMEM((half + 1, tile, f_out), BF16),
            pltpu.VMEM((half + 1, tile, f_out), BF16),
            pltpu.VMEM((2, nz, tile, f_out), BF16),
            pltpu.VMEM((n_row, tile, f_out), BF16),
            pltpu.VMEM((n_row, tile, f_out), BF16),
            pltpu.VMEM((n_plane, 2 * chunk, f_out), F32),
            pltpu.VMEM((n_plane, 2 * chunk, f_out), F32),
            pltpu.VMEM((near_n, 2 * chunk, f_out), F32),
            pltpu.VMEM((far_n, 2 * chunk, f_out), F32),
            pltpu.VMEM((n_plane, chunk, f_out), F32),
            pltpu.SMEM((slots,), jnp.int32),
            pltpu.SMEM((slots,), jnp.int32),
            pltpu.SMEM((n_col,), jnp.int32),
            pltpu.SMEM((n_row,), jnp.int32),
            dma((5,)),
            dma((n_row,)),
            dma((n_row,)),
            dma((2 * parts,)),
            dma((2 * parts,)),
            dma,
            dma((half + 1,)),
            dma,
            dma((half + 1,)),
            dma,
            dma((half + 1,)),
            dma,
            dma((half + 1,)),
            dma,
            dma,
            dma((n_row,)),
            dma((n_row,)),
            dma((n_plane,)),
            dma((n_plane,)),
            dma((near_n,)),
            dma((near_n,)),
            dma((far_n,)),
            dma((far_n,)),
            dma((n_plane,)),
            dma((n_plane,)),
        ],
        compiler_params=pltpu.CompilerParams(
            collective_id=0, has_side_effects=True, vmem_limit_bytes=48 * 1024 * 1024
        ),
    )(
        where.reshape(slots),
        live.reshape(1),
        features,
        weight,
        bias.reshape(1, f_out),
        cotangent,
        tiles.reshape(slots, tile, tile),
    )
    return (
        hidden,
        grad_features,
        grad_weight.reshape(f_in, f_out),
        grad_bias.reshape(f_out),
    )


def solution(mesh):
    placed = (
        P(("col", "row"), None),
        P(),
        P(),
        P("row", "col", None, None, None),
        P("row", "col", None),
        P("row", "col"),
        P(("row", "col"), None),
    )
    return jax.shard_map(
        functools.partial(local, mesh.shape["row"], mesh.shape["col"]),
        mesh=mesh,
        in_specs=placed,
        out_specs=(P(("row", "col"), None), P(("col", "row"), None), P(), P()),
        check_vma=False,
    )
```

```python
import functools
import math

import jax
import jax.numpy as jnp
from jax import lax
from jax.experimental import pallas as pl
from jax.experimental.pallas import tpu as pltpu
from jax.sharding import PartitionSpec as P

F32, BF16 = jnp.float32, jnp.bfloat16
HIGHEST = lax.Precision.HIGHEST


def plan(nz):
    half = nz // 2
    stride = 4 if half % 4 == 0 and half > 4 else 2
    near_n = 8 if nz % 8 == 0 and nz > 8 else 2
    return half, stride, half // stride, near_n, nz // near_n


def plane_steps(n_row):
    width = 4 if n_row % 4 == 0 else n_row
    height = n_row // width

    def hops(step):
        down, across = step
        return min(down, height - down) + min(across, width - across)

    steps = [(down, across) for down in range(height) for across in range(width)]
    return width, sorted(steps, key=hops, reverse=True)[:-1]


def gelu_parts(values):
    normal_cdf = 0.5 * (1.0 + lax.erf(values * 0.7071067811865476))
    density = jnp.exp(-0.5 * values * values) * 0.3989422804014327
    return (values * normal_cdf, normal_cdf + values * density)


def layer(
    n_row,
    nz,
    scaling,
    where,
    live,
    features_hbm,
    weight_hbm,
    bias_hbm,
    cotangent_hbm,
    tiles_hbm,
    hidden_out,
    grad_features_out,
    grad_weight_out,
    grad_bias_out,
    features,
    weight,
    bias,
    cotangent,
    tiles,
    tiles_t,
    features_t,
    panel,
    products,
    compact,
    to_sib,
    from_sib,
    up,
    down,
    up_in,
    down_in,
    grads,
    back,
    back_in,
    terms,
    terms_in,
    near,
    far,
    total,
    prev_row,
    prev_col,
    last_row,
    last_col,
    load_sem,
    panel_send,
    panel_recv,
    features_send,
    features_recv,
    sib_send,
    sib_recv,
    up_send,
    up_recv,
    down_send,
    down_recv,
    right_send,
    right_recv,
    left_send,
    left_recv,
    pass_send,
    pass_recv,
    back_send,
    back_recv,
    terms_send,
    terms_recv,
    near_send,
    near_recv,
    far_send,
    far_recv,
    total_send,
    total_recv,
):
    slots, tile = tiles.shape[0], tiles.shape[1]
    row, col = lax.axis_index("row"), lax.axis_index("col")
    z, core = col // 2, col % 2
    half, stride, levels, near_n, far_n = plan(nz)
    n_plane = 2 * n_row
    place = 2 * row + core
    width_x, steps = plane_steps(n_row)
    group, spot = z // near_n, z % near_n

    def device(at_row, at_z, at_core):
        return (at_row, 2 * at_z + at_core)

    def remote(src, dst, send, recv, to):
        return pltpu.make_async_remote_copy(
            src_ref=src,
            dst_ref=dst,
            send_sem=send,
            recv_sem=recv,
            device_id=to,
            device_id_type=pl.DeviceIdType.MESH,
        )

    def settle(ref, sem):
        pltpu.make_async_copy(ref, ref, sem).wait()

    def above(hop):
        return device(row, (z + hop) % nz, core)

    def below(hop):
        return device(row, (z + nz - hop) % nz, core)

    sibling = device(row, z, 1 - core)

    def plane(step):
        other = (place + step) % n_plane
        return device(other // 2, z, other % 2), other

    def peer(step):
        down, across = step
        return (row // width_x + down) % (n_row // width_x) * width_x + (
            row + across
        ) % width_x

    barrier = pltpu.get_barrier_semaphore()

    def greet(to):
        pl.semaphore_signal(
            barrier, inc=1, device_id=to, device_id_type=pl.DeviceIdType.MESH
        )

    for hop in range(stride, 0, -1):
        greet(above(hop))
        greet(below(hop))

    for step in steps:
        greet(device(peer(step), z, core))
    greet(sibling)

    loads = [
        pltpu.make_async_copy(src, dst, load_sem.at[at])
        for at, (src, dst) in enumerate(
            (
                (features_hbm, features),
                (weight_hbm, weight),
                (tiles_hbm, tiles),
                (bias_hbm, bias),
                (cotangent_hbm, cotangent),
            )
        )
    ]
    for load in loads:
        load.start()
    loads[0].wait()
    loads[1].wait()
    panel[row] = jnp.dot(
        features[...], weight[...], precision=HIGHEST, preferred_element_type=F32
    ).astype(BF16)
    pl.semaphore_wait(barrier, n_row + 2 * stride)

    def panel_copy(at):
        return remote(
            panel.at[row],
            panel.at[row],
            panel_send,
            panel_recv,
            device(peer(steps[at]), z, core),
        )

    for at in range(n_row - 1):
        panel_copy(at).start()

    count = live[0]
    n_cols = n_row

    @pl.loop(0, slots)
    def _(slot):
        mine = where[slot]
        by_row, by_col = jnp.int32(slots), jnp.int32(slots)
        for other in range(slots):
            theirs = where[other]
            before = other < slot
            by_row = jnp.where(
                before & (theirs // n_cols == mine // n_cols), other, by_row
            )
            by_col = jnp.where(
                before & (theirs % n_cols == mine % n_cols), other, by_col
            )
        prev_row[slot] = by_row
        prev_col[slot] = by_col

    @pl.loop(0, 2 * nz)
    def _(tile_row):
        last = jnp.int32(slots)
        for other in range(slots):
            last = jnp.where(
                (other < count) & (where[other] // n_cols == tile_row), other, last
            )
        last_row[tile_row] = last

    @pl.loop(0, n_cols)
    def _(tile_col):
        last = jnp.int32(slots)
        for other in range(slots):
            last = jnp.where(
                (other < count) & (where[other] % n_cols == tile_col), other, last
            )
        last_col[tile_col] = last

    products[slots] = jnp.zeros_like(products[slots])
    compact[slots] = jnp.zeros_like(compact[slots])
    for load in loads[2:]:
        load.wait()

    settle(panel.at[pl.ds(0, n_row - 1)], panel_recv)

    for slot in range(slots):
        products[slot] = jnp.dot(
            tiles[slot], panel[where[slot] % n_cols], preferred_element_type=F32
        )

    @pl.loop(0, slots)
    def _(slot):
        added = products[slot] + products[prev_row[slot]]
        products[slot] = added
        compact[slot] = added.astype(BF16)

    parts, width = levels, stride

    def sib_copies(part):
        for end, first in enumerate((part * width, nz - width - part * width)):
            yield remote(
                to_sib.at[pl.ds(first, width)],
                from_sib.at[pl.ds(first, width)],
                sib_send,
                sib_recv.at[2 * part + end],
                sibling,
            )

    def slot_of(at, whose):
        return last_row[2 * ((z + at + nz - (half - 1)) % nz) + whose]

    for part in range(parts):

        @pl.loop(part * width, (part + 1) * width)
        def _(at):
            to_sib[at] = compact[slot_of(at, 1 - core)]
            to_sib[nz - 1 - at] = compact[slot_of(nz - 1 - at, 1 - core)]

        for copy in sib_copies(part):
            copy.start()

    def up_copy(dist):
        to = above(dist % stride or stride)
        return remote(up.at[dist], up_in.at[dist], up_send, up_recv.at[dist], to)

    def down_copy(dist):
        to = below(dist % stride or stride)
        return remote(
            down.at[dist], down_in.at[dist], down_send, down_recv.at[dist], to
        )

    def chip_part(dist):
        at = half - 1 + dist
        return compact[slot_of(at, core)].astype(F32) + from_sib[at].astype(F32)

    def send_up(dist, value):
        up[dist] = value.astype(BF16)
        up_copy(dist).start()

    def send_down(dist, value):
        down[dist] = value.astype(BF16)
        down_copy(dist).start()

    def fill(level):
        for copy in sib_copies(levels - 1 - level):
            copy.wait_recv()
        if level == levels - 1:
            send_up(half, chip_part(half))
        for hop in range(stride - 1, 0, -1):
            dist = level * stride + hop
            send_down(dist, chip_part(-dist))
            send_up(dist, chip_part(dist))

    def gather_up(level, value):
        for dist in range(level * stride + 1, (level + 1) * stride + 1):
            up_copy(dist).wait_recv()
            value = value + up_in[dist].astype(F32)
        return value

    def gather_down(level, value):
        for dist in range(level * stride + 1, min((level + 1) * stride, half - 1) + 1):
            down_copy(dist).wait_recv()
            value = value + down_in[dist].astype(F32)
        return value

    fill(levels - 1)
    fill(levels - 2)

    features_t[:, pl.ds(pl.multiple_of(row * tile, tile), tile)] = (
        features[...].T.astype(BF16)
    )

    def features_copy(at):
        mine = features_t.at[:, pl.ds(pl.multiple_of(row * tile, tile), tile)]
        return remote(
            mine,
            mine,
            features_send,
            features_recv,
            device(peer(steps[at]), z, core),
        )

    for at in range(n_row - 1):
        features_copy(at).start()

    for level in range(levels - 1, 0, -1):
        dist = level * stride
        send_up(dist, gather_up(level, chip_part(dist)))
        send_down(dist, gather_down(level, chip_part(-dist)))
        if level > 1:
            fill(level - 2)

    own = products[slot_of(half - 1, core)] + from_sib[half - 1].astype(F32)
    preact = gather_up(0, gather_down(0, own + bias[...]))
    hidden, slopes = gelu_parts(preact)
    grad_preact = cotangent[...] * slopes
    grads[core, z] = grad_preact.astype(BF16)

    def right_copy(level, hop):
        at = grads.at[core, (z + nz - level * stride) % nz]
        sem = right_recv.at[level * stride + hop]
        return remote(at, at, right_send, sem, above(hop))

    def left_copy(level, hop):
        at = grads.at[core, (z + level * stride) % nz]
        sem = left_recv.at[level * stride + hop]
        return remote(at, at, left_send, sem, below(hop))

    def pass_copy(at_z):
        at = grads.at[core, at_z]
        return remote(at, at, pass_send, pass_recv, sibling)

    def from_left(dist):
        at = (z + nz - dist) % nz
        settle(grads.at[core, at], right_recv.at[dist])
        return at

    def from_right(dist):
        at = (z + dist) % nz
        settle(grads.at[core, at], left_recv.at[dist])
        return at

    right_copy(0, stride).start()
    left_copy(0, stride).start()
    pass_copy(z).start()

    def serve_between(level):
        for hop in range(stride - 1, 0, -1):
            right_copy(level, hop).start()
            left_copy(level, hop).start()

    serve_between(0)
    hidden_out[...] = hidden
    rows_dev, width_out = grad_preact.shape
    bias_term = jnp.sum(grad_preact.reshape(rows_dev // 8, 8, width_out), axis=0)

    @pl.loop(0, n_plane)
    def _(at):
        terms[at, 8:16] = bias_term

    @pl.loop(0, slots)
    def _(slot):
        tiles_t[slot] = tiles[slot].T


    for level in range(1, levels + 1):
        relayed = [from_left(level * stride)]
        if level < levels:
            right_copy(level, stride).start()
            relayed.append(from_right(level * stride))
            if level < levels - 1:
                left_copy(level, stride).start()
        for at in relayed:
            pass_copy(at).start()
        if level < levels:
            serve_between(level)
        for hop in range(1, stride):
            dist = (level - 1) * stride + hop
            pass_copy(from_left(dist)).start()
            pass_copy(from_right(dist)).start()

    settle(grads.at[1 - core], pass_recv)

    for slot in range(slots):
        tile_row = where[slot] // n_cols
        products[slot] = jnp.dot(
            tiles_t[slot],
            grads[tile_row % 2, tile_row // 2],
            preferred_element_type=F32,
        )

    @pl.loop(0, slots)
    def _(slot):
        products[slot] = products[slot] + products[prev_col[slot]]

    for at in range(n_row):
        back[at * tile : (at + 1) * tile] = products[last_col[at]].astype(BF16)

    features_but_own = features_t.at[:, pl.ds(0, (n_row - 1) * tile)]
    settle(features_but_own, features_recv)
    weight_term = jnp.dot(features_t[...], back[...], preferred_element_type=F32)
    for at in range(n_plane):
        terms[at, 0:8] = weight_term[8 * at : 8 * at + 8]

    def terms_copy(step):
        to, other = plane(step)
        return remote(
            terms.at[other],
            terms_in.at[place],
            terms_send,
            terms_recv,
            to,
        )

    @pl.loop(1, n_plane)
    def _(step):
        terms_copy(step).start()

    def back_copy(at):
        to = peer(steps[at])
        return remote(
            back.at[pl.ds(pl.multiple_of(to * tile, tile), tile)],
            back_in.at[at],
            back_send,
            back_recv,
            device(to, z, core),
        )

    terms_in[place] = terms[place]

    settle(terms_in.at[pl.ds(0, n_plane - 1)], terms_recv)
    near[spot] = lax.fori_loop(
        1, n_plane, lambda at, so_far: so_far + terms_in[at], terms_in[0]
    )

    def near_copy(step):
        at = near.at[spot]
        to = device(row, group * near_n + (spot + step) % near_n, core)
        return remote(at, at, near_send, near_recv, to)

    def far_copy(step):
        at = far.at[group]
        to = above(near_n * step)
        return remote(at, at, far_send, far_recv, to)

    for step in range(1, near_n):
        near_copy(step).start()
    for at in range(n_row - 1):
        back_copy(at).start()
    settle(near.at[pl.ds(0, near_n - 1)], near_recv)
    far[group] = sum((near[at] for at in range(1, near_n)), near[0])
    for step in range(1, far_n):
        far_copy(step).start()

    mine = back[pl.ds(pl.multiple_of(row * tile, tile), tile)]
    grad_product = mine.astype(F32)
    settle(back_in.at[pl.ds(0, n_row - 1)], back_recv)
    for at in range(n_row - 1):
        grad_product = grad_product + back_in[at].astype(F32)
    grad_features_out[...] = lax.dot_general(
        grad_product,
        weight[...],
        (((1,), (1,)), ((), ())),
        precision=HIGHEST,
        preferred_element_type=F32,
    )

    settle(far.at[pl.ds(0, far_n - 1)], far_recv)
    summed = sum((far[at] for at in range(1, far_n)), far[0]) * scaling
    total[place] = summed[0:8]

    def total_copy(step):
        return remote(
            total.at[place],
            total.at[place],
            total_send,
            total_recv,
            plane(step)[0],
        )

    @pl.loop(1, n_plane)
    def _(step):
        total_copy(step).start()

    grad_bias_out[...] = jnp.sum(summed[8:16], axis=0, keepdims=True)

    settle(panel.at[pl.ds(0, n_row - 1)], panel_send)
    settle(features_but_own, features_send)
    settle(back_in.at[pl.ds(0, n_row - 1)], back_send)
    settle(to_sib, sib_send)
    settle(up.at[pl.ds(1, half)], up_send)
    settle(down.at[pl.ds(1, half - 1)], down_send)
    settle(grads.at[0, pl.ds(0, half)], right_send)
    settle(grads.at[0, pl.ds(0, half - 1)], left_send)
    settle(grads.at[0], pass_send)
    settle(terms_in.at[pl.ds(0, n_plane - 1)], terms_send)
    settle(near.at[pl.ds(0, near_n - 1)], near_send)
    settle(far.at[pl.ds(0, far_n - 1)], far_send)
    settle(total.at[pl.ds(0, n_plane - 1)], total_send)
    settle(total.at[pl.ds(0, n_plane - 1)], total_recv)
    grad_weight_out[...] = total[...]


def local(n_row, n_col, features, weight, bias, tiles, where, live, cotangent):
    slots, tile = tiles.shape[2], tiles.shape[3]
    rows_dev, f_in = features.shape
    f_out = weight.shape[1]
    nz = n_col // 2
    half, stride, levels, near_n, far_n = plan(nz)
    n_plane = 2 * n_row
    parts = levels
    nodes = rows_dev * n_row * n_col
    chunk = f_in // n_plane
    assert chunk == 8 and rows_dev == tile
    dma = pltpu.SemaphoreType.DMA
    vmem = pl.BlockSpec(memory_space=pltpu.VMEM)
    smem = pl.BlockSpec(memory_space=pltpu.SMEM)
    hidden, grad_features, grad_weight, grad_bias = pl.pallas_call(
        functools.partial(layer, n_row, nz, 1.0 / math.sqrt(nodes)),
        out_shape=(
            jax.ShapeDtypeStruct((rows_dev, f_out), F32),
            jax.ShapeDtypeStruct((rows_dev, f_in), F32),
            jax.ShapeDtypeStruct((n_plane, chunk, f_out), F32),
            jax.ShapeDtypeStruct((1, f_out), F32),
        ),
        in_specs=[smem, smem] + [pl.BlockSpec(memory_space=pltpu.HBM)] * 5,
        out_specs=(vmem, vmem, vmem, vmem),
        scratch_shapes=[
            pltpu.VMEM(features.shape, F32),
            pltpu.VMEM(weight.shape, F32),
            pltpu.VMEM((1, f_out), F32),
            pltpu.VMEM(cotangent.shape, F32),
            pltpu.VMEM((slots, tile, tile), BF16),
            pltpu.VMEM((slots, tile, tile), BF16),
            pltpu.VMEM((f_in, n_row * rows_dev), BF16),
            pltpu.VMEM((n_row, tile, f_out), BF16),
            pltpu.VMEM((slots + 1, tile, f_out), F32),
            pltpu.VMEM((slots + 1, tile, f_out), BF16),
            pltpu.VMEM((nz, tile, f_out), BF16),
            pltpu.VMEM((nz, tile, f_out), BF16),
            pltpu.VMEM((half + 1, tile, f_out), BF16),
            pltpu.VMEM((half + 1, tile, f_out), BF16),
            pltpu.VMEM((half + 1, tile, f_out), BF16),
            pltpu.VMEM((half + 1, tile, f_out), BF16),
            pltpu.VMEM((2, nz, tile, f_out), BF16),
            pltpu.VMEM((n_row * tile, f_out), BF16),
            pltpu.VMEM((n_row, tile, f_out), BF16),
            pltpu.VMEM((n_plane, 2 * chunk, f_out), F32),
            pltpu.VMEM((n_plane, 2 * chunk, f_out), F32),
            pltpu.VMEM((near_n, 2 * chunk, f_out), F32),
            pltpu.VMEM((far_n, 2 * chunk, f_out), F32),
            pltpu.VMEM((n_plane, chunk, f_out), F32),
            pltpu.SMEM((slots,), jnp.int32),
            pltpu.SMEM((slots,), jnp.int32),
            pltpu.SMEM((n_col,), jnp.int32),
            pltpu.SMEM((n_row,), jnp.int32),
            dma((5,)),
            dma,
            dma,
            dma,
            dma,
            dma,
            dma((2 * parts,)),
            dma,
            dma((half + 1,)),
            dma,
            dma((half + 1,)),
            dma,
            dma((half + 1,)),
            dma,
            dma((half + 1,)),
            dma,
            dma,
            dma,
            dma,
            dma,
            dma,
            dma,
            dma,
            dma,
            dma,
            dma,
            dma,
        ],
        compiler_params=pltpu.CompilerParams(
            collective_id=0, has_side_effects=True, vmem_limit_bytes=56 * 1024 * 1024
        ),
    )(
        where.reshape(slots),
        live.reshape(1),
        features,
        weight,
        bias.reshape(1, f_out),
        cotangent,
        tiles.reshape(slots, tile, tile),
    )
    return (
        hidden,
        grad_features,
        grad_weight.reshape(f_in, f_out),
        grad_bias.reshape(f_out),
    )


def solution(mesh):
    placed = (
        P(("col", "row"), None),
        P(),
        P(),
        P("row", "col", None, None, None),
        P("row", "col", None),
        P("row", "col"),
        P(("row", "col"), None),
    )
    return jax.shard_map(
        functools.partial(local, mesh.shape["row"], mesh.shape["col"]),
        mesh=mesh,
        in_specs=placed,
        out_specs=(P(("row", "col"), None), P(("col", "row"), None), P(), P()),
        check_vma=False,
    )
```
